256 devices in a mesh: tok: 64 (over x, z_lo, y), proj: 4 (over z_hi, core).
Axes of the slice: x: 4, y: 4, z: 8 (z_hi: 2, z_lo: 4; z = z_hi * 4 + z_lo), core: 2. Of those that a mesh axis runs over, the one named last changes fastest.
Arguments:
- latent: bfloat16 [65536, 512], P('tok', 'proj'), may hold values from -400 to 400
- grad_key: bfloat16 [65536, 2048], P('tok', 'proj'), may hold values from -400 to 400
- grad_value: bfloat16 [65536, 2048], P('tok', 'proj'), may hold values from -400 to 400
Outputs:
- latent_cov: float32 [512, 512], P(None, 'proj')
- key_cov: float32 [2048, 2048], P('tok', 'proj')
- value_cov: float32 [2048, 2048], P('tok', 'proj')
The draws below stay inside these ranges and needn't reach their ends.
All inputs are finite; a program needn't handle non-finite values.
Results may differ from the reference program's by a relative error of at most 0.0003.
Values may be sent and summed in bfloat16 or wider, within the bound.
No kernel may reach another device: no remote copies, remote signals or barrier semaphores. Data moves between devices by JAX's collectives and lax.ppermute only.
A program may use at most 64 MiB of HBM per device.

```python
import math
import jax
import jax.numpy as jnp
from jax import lax

LATENT = 512
HEADS = 16
HEAD_DIM = 128
TOKENS = 65536


def make_field(key, rows, cols, row_low, row_high):
    first, second, third = jax.random.split(key, 3)
    base = jax.random.truncated_normal(first, -4.0, 4.0, (rows, cols), jnp.float32)
    mixed = base + 0.6 * jnp.roll(base, 1, axis=1) - 0.4 * jnp.roll(base, 5, axis=1)
    column_scale = jnp.exp(jax.random.uniform(second, (1, cols), jnp.float32, 0.0, math.log(10.0))) / 3.16
    position = jnp.arange(rows, dtype=jnp.float32)[:, None] / rows
    row_scale = jnp.exp(jax.random.uniform(third, (rows, 1), jnp.float32, math.log(row_low), math.log(row_high)))
    row_scale = row_scale * jnp.exp(math.log(3.0) * position)
    return (mixed * column_scale * row_scale / 1.3).astype(jnp.float32)


def draw_latent(key, part):
    key = jax.random.fold_in(key, 11)
    return make_field(key, TOKENS, LATENT, 0.6, 1.6).astype(jnp.bfloat16)


def draw_grad_key(key, part):
    key = jax.random.fold_in(key, 12)
    return make_field(key, TOKENS, HEADS * HEAD_DIM, 0.6, 1.6).astype(jnp.bfloat16)


def draw_grad_value(key, part):
    key = jax.random.fold_in(key, 13)
    return make_field(key, TOKENS, HEADS * HEAD_DIM, 0.6, 1.6).astype(jnp.bfloat16)


def setup_inputs(seed: int = 0) -> dict:
    arg_keys = jax.random.split(jax.random.key(seed), 4)
    return {
        "latent": draw_latent(jax.random.fold_in(arg_keys[3], 71), 0),
        "grad_key": draw_grad_key(jax.random.fold_in(arg_keys[3], 71), 0),
        "grad_value": draw_grad_value(jax.random.fold_in(arg_keys[3], 71), 0),
    }


def covariance(values):
    wide = values.astype(jnp.float32)
    total = lax.dot_general(wide, wide, (((0,), (0,)), ((), ())), precision=lax.Precision.HIGHEST, preferred_element_type=jnp.float32)
    return total / jnp.float32(TOKENS)


def reference(latent, grad_key, grad_value):
    return covariance(latent), covariance(grad_key), covariance(grad_value)
```

```python
import functools
import itertools

import jax
import jax.numpy as jnp
from jax import lax
from jax.experimental import pallas as pl
from jax.experimental.pallas import tpu as pltpu
from jax.sharding import Mesh, PartitionSpec as P

AXES = ("x", "zl", "y", "zh", "core")
SIZES = (4, 4, 4, 2, 2)
CHUNKS = (1, 2, 1)
F32 = jnp.float32


def move(values, where):
    pairs = []
    for source, place in enumerate(itertools.product(*[range(n) for n in SIZES])):
        target = where(*place)
        if target is None:
            continue
        index = 0
        for n, t in zip(SIZES, target):
            index = index * n + t % n
        pairs.append((source, index))
    return lax.ppermute(values, AXES, pairs)


def to_core(x, zl, y, zh, core):
    return (x, zl, y, zh, 1 - core)


def to_half(x, zl, y, zh, core):
    return (x, zl, y, 1 - zh, core)


def first(step):
    return lambda x, zl, y, zh, core: (
        (x + step, zl, y, zh, core) if core == 0 else (x, zl, y + step, zh, core)
    )


def second(step):
    return lambda x, zl, y, zh, core: (
        (x, zl, y + step, zh, core) if core == 0 else (x + step, zl, y, zh, core)
    )


def along_z(step):
    return lambda x, zl, y, zh, core: (x, zl + step, y, zh, core)


def crossing(x, zl, y, zh, core):
    return (x, zl, y, 1 - zh, core) if x // 2 == zh else None


def value_home(x, zl, y, zh, core):
    return (x + 2, zl, y, zh, core) if x // 2 != zh else None


def product(left, right):
    return lax.dot_general(left, right, (((0,), (0,)), ((), ())), preferred_element_type=F32)


def block_of(kind, zh, core):
    half = zh if kind < 2 else 1 - zh
    return 2 * half + (core if kind % 2 == 0 else 1 - core)


def place(scalars, kind, zl, yb):
    x, y, zh, core = scalars[0], scalars[1], scalars[3], scalars[4]
    jx = lax.rem(block_of(kind, zh, core) - x + 4, 4)
    jy = lax.rem(yb - y + 4, 4)
    is0 = core == 0
    return (
        jnp.where(is0, jx, jy),
        jnp.where(is0, zl, kind),
        jnp.where(is0, yb, zl),
    )


def emit(room, outs, sems):
    copies = [pltpu.make_async_copy(room.at[j], outs[j], sems.at[j]) for j in range(4)]
    for c in copies:
        c.start()
    for c in copies:
        c.wait()


def own_kernel(scalars, km, ko, vm, vo, lm, lo, lf, lfo, o0, o1, o2, o3, room, sems):
    for kind, (left, right) in enumerate([(km, km), (ko, km), (vm, vm), (vo, vm)]):
        for zl in range(4):
            block = product(left[:, 128 * zl : 128 * (zl + 1)], right[...])
            for yb in range(4):
                i0, i1, i2 = place(scalars, kind, zl, yb)
                for cg in range(4):
                    room[i0, i1, i2, 32 * cg : 32 * (cg + 1), :] = block[
                        32 * yb : 32 * (yb + 1), 128 * cg : 128 * (cg + 1)
                    ]
    for kind, left in enumerate([lm, lo, lf, lfo]):
        block = product(left[...], lm[...])
        for zl in range(4):
            for yb in range(4):
                i0, i1, i2 = place(scalars, kind, zl, yb)
                row = 32 * zl + 8 * yb
                room[i0, i1, i2, 128:136, :] = block[row : row + 8, :]
    emit(room, (o0, o1, o2, o3), sems)


def cross_kernel(quarters, scalars, nm, no, fm, fo, o0, o1, o2, o3, room, sems):
    for kind, left in enumerate([nm, no]):
        for zl in range(4):
            block = product(left[:, 128 * zl : 128 * (zl + 1)], fm[...])
            for yb in range(4):
                i0, i1, i2 = place(scalars, kind, zl, yb)
                for e in range(quarters):
                    room[i0, i1, i2, 32 * e : 32 * (e + 1), :] = block[
                        32 * yb : 32 * (yb + 1), 128 * e : 128 * (e + 1)
                    ]
    for kind, left in enumerate([fm, fo]):
        for e in range(quarters):
            block = product(left[:, 128 * e : 128 * (e + 1)], nm[...])
            for zl in range(4):
                for yb in range(4):
                    i0, i1, i2 = place(scalars, kind + 2, zl, yb)
                    row = 32 * zl + 8 * yb
                    for cg in range(4):
                        at = 32 * e + 8 * cg
                        room[i0, i1, i2, at : at + 8, :] = block[
                            row : row + 8, 128 * cg : 128 * (cg + 1)
                        ]
    emit(room, (o0, o1, o2, o3), sems)


def middle_kernel(scalars, a, b, c, d, o0, o1, o2, o3):
    x, y, zh, core = scalars[0], scalars[1], scalars[3], scalars[4]
    is0 = core == 0
    for j, out in enumerate((o0, o1, o2, o3)):
        yb = lax.rem(y + j, 4)
        xb = lax.rem(x + j, 4)
        kind = 2 * jnp.where(xb // 2 == zh, 0, 1) + jnp.where(xb % 2 == core, 0, 1)
        for slab in range(4):
            i = jnp.where(is0, slab, kind)
            k = jnp.where(is0, yb, slab)
            out[slab] = (a[i, k] + b[i, k]) + (c[i, k] + d[i, k])


def last_kernel(scalars, a, b, c, d, o0, o1, o2, o3):
    zl = scalars[2]
    for j, out in enumerate((o0, o1, o2, o3)):
        i = lax.rem(zl + j, 4)
        out[...] = (a[i] + b[i]) + (c[i] + d[i])


SMEM = pl.BlockSpec(memory_space=pltpu.SMEM)
VMEM = pl.BlockSpec(memory_space=pltpu.VMEM)
ANY = pl.BlockSpec(memory_space=pl.ANY)


def blocks_call(kernel, rows, scalars, *operands):
    shape = (4, 4, rows, 128)
    flops = 2 * 1024 * 16 * 4 * rows * 128
    return pl.pallas_call(
        kernel,
        out_shape=[jax.ShapeDtypeStruct(shape, F32)] * 4,
        in_specs=[SMEM] + [VMEM] * len(operands),
        out_specs=[ANY] * 4,
        scratch_shapes=[pltpu.VMEM((4,) + shape, F32), pltpu.SemaphoreType.DMA((4,))],
        compiler_params=pltpu.CompilerParams(vmem_limit_bytes=40 * 2**20),
        cost_estimate=pl.CostEstimate(flops=flops, bytes_accessed=4 * 16 * rows * 512, transcendentals=0),
    )(scalars, *operands)


def sums_call(kernel, shape, scalars, operands):
    count = 4
    for n in shape:
        count *= n
    return pl.pallas_call(
        kernel,
        out_shape=[jax.ShapeDtypeStruct(shape, F32)] * 4,
        in_specs=[SMEM] + [VMEM] * 4,
        out_specs=[VMEM] * 4,
        compiler_params=pltpu.CompilerParams(vmem_limit_bytes=40 * 2**20),
        cost_estimate=pl.CostEstimate(flops=4 * count, bytes_accessed=20 * count, transcendentals=0),
    )(scalars, *operands)


def exchange(parts, direction):
    return [parts[0]] + [move(parts[j], direction(j)) for j in (1, 2, 3)]


def shards(latent, grad_key, grad_value):
    x, zl, y, zh, core = (lax.axis_index(a) for a in AXES)
    scalars = jnp.stack([x, y, zl, zh, core]).astype(jnp.int32)
    scale = F32(1.0 / (latent.shape[0] * 64))
    width = grad_key.shape[1]
    low = zh == 0

    to = jnp.arange(width)
    source = 128 * ((to // 32) % 4) + 32 * ((to // 8) % 4) + 8 * (to // 128) + to % 8
    chosen = jnp.where(low, grad_value, grad_key)
    latent_far = move(latent, to_half)
    far, start = [], 0
    for quarters in CHUNKS:
        pick = (jnp.arange(width)[:, None] == source[None, start : start + 128 * quarters])
        part = jnp.dot(chosen, pick.astype(jnp.bfloat16), preferred_element_type=F32)
        far.append(move(part.astype(jnp.bfloat16), to_half))
        start += 128 * quarters

    key_other = move(grad_key, to_core)
    value_other = move(grad_value, to_core)
    latent_other = move(latent, to_core)
    near = jnp.where(low, grad_key, grad_value)
    near_other = jnp.where(low, key_other, value_other)
    latent_far_other = move(latent_far, to_core)

    own = blocks_call(
        own_kernel, 136, scalars, grad_key, key_other, grad_value, value_other,
        latent, latent_other, latent_far, latent_far_other,
    )
    own = exchange(own, first)
    own = sums_call(middle_kernel, (4, 136, 128), scalars, own)
    own = exchange(own, second)
    own = sums_call(last_kernel, (136, 128), scalars, own)
    own = exchange(own, along_z)
    own = (own[0] + own[1]) + (own[2] + own[3])
    piece = own[128:136]
    own = own[:128]
    own_moved = move(own, value_home)

    pieces = []
    for index, quarters in enumerate(CHUNKS):
        rows = 32 * quarters
        mine = far[index]
        other = move(mine, to_core)
        part = blocks_call(
            functools.partial(cross_kernel, quarters), rows, scalars, near, near_other, mine, other
        )
        part = exchange(part, first)
        part = sums_call(middle_kernel, (4, rows, 128), scalars, part)
        part = exchange(part, second)
        part = sums_call(last_kernel, (rows, 128), scalars, part)
        part = exchange(part, along_z)
        pieces.append((part[0] + part[1]) + (part[2] + part[3]))
    cross = jnp.concatenate(pieces, axis=0)
    cross_moved = move(cross, crossing)

    back = cross_moved.reshape(4, 32, 128).swapaxes(0, 1).reshape(32, width)
    place_back = (source[:, None] == jnp.arange(width)[None, :]).astype(F32)
    back = jnp.dot(back, place_back, precision=lax.Precision.HIGHEST)
    stay = cross.reshape(4, 4, 8, 128).swapaxes(1, 2).reshape(32, width)
    own_key = own.reshape(4, 32, 128).swapaxes(0, 1).reshape(32, width)
    own_value = own_moved.reshape(4, 32, 128).swapaxes(0, 1).reshape(32, width)

    def gather(values, direction, position):
        got = [values] + [move(values, direction(j)) for j in (1, 2, 3)]
        return jnp.stack([lax.select_n((position - b + 4) % 4, *got) for b in range(4)])

    piece = gather(piece, along_z, zl)
    piece = gather(piece, second, jnp.where(core == 0, y, x))
    piece = gather(piece, first, jnp.where(core == 0, x, y))
    piece = jnp.where(core == 0, piece, piece.swapaxes(0, 1))
    latent_sum = piece.swapaxes(1, 2).reshape(512, 128)

    inside = (x // 2) == zh
    key_sum = jnp.where(inside, own_key, jnp.where(low, stay, back))
    value_sum = jnp.where(inside, own_value, jnp.where(low, back, stay))
    return latent_sum * scale, key_sum * scale, value_sum * scale


def solution(mesh):
    fine = Mesh(mesh.devices.reshape(SIZES), AXES)
    tok, proj = ("x", "zl", "y"), ("zh", "core")
    placed = (P(tok, proj), P(tok, proj), P(tok, proj))
    return jax.shard_map(
        shards,
        mesh=fine,
        in_specs=placed,
        out_specs=(P(None, proj), P(tok, proj), P(tok, proj)),
        check_vma=False,
    )
```

```python
import functools
import itertools

import jax
import jax.numpy as jnp
from jax import lax
from jax.experimental import pallas as pl
from jax.experimental.pallas import tpu as pltpu
from jax.sharding import Mesh, PartitionSpec as P

AXES = ("x", "zl", "y", "zh", "core")
SIZES = (4, 4, 4, 2, 2)
CHUNKS = (1, 3)
F32 = jnp.float32


def move(values, where):
    pairs = []
    for source, place in enumerate(itertools.product(*[range(n) for n in SIZES])):
        target = where(*place)
        if target is None:
            continue
        index = 0
        for n, t in zip(SIZES, target):
            index = index * n + t % n
        pairs.append((source, index))
    return lax.ppermute(values, AXES, pairs)


def to_core(x, zl, y, zh, core):
    return (x, zl, y, zh, 1 - core)


def to_half(x, zl, y, zh, core):
    return (x, zl, y, 1 - zh, core)


def first(step):
    return lambda x, zl, y, zh, core: (
        (x + step, zl, y, zh, core) if core == 0 else (x, zl, y + step, zh, core)
    )


def second(step):
    return lambda x, zl, y, zh, core: (
        (x, zl, y + step, zh, core) if core == 0 else (x + step, zl, y, zh, core)
    )


def along_z(step):
    return lambda x, zl, y, zh, core: (x, zl + step, y, zh, core)


def homeward(x, zl, y, zh, core):
    return (x, zl, y, 1 - zh, core) if x // 2 == zh else (x + 2, zl, y, zh, core)


def sideways(x, zl, y, zh, core):
    return (x ^ 1, zl, y, zh, 1 - core) if x // 2 != zh and x % 2 != core else None


def product(left, right):
    return lax.dot_general(left, right, (((0,), (0,)), ((), ())), preferred_element_type=F32)


def block_of(kind, zh, core):
    half = zh if kind < 2 else 1 - zh
    return 2 * half + (core if kind % 2 == 0 else 1 - core)


def place(scalars, kind, zl, yb):
    x, y, zh, core = scalars[0], scalars[1], scalars[3], scalars[4]
    jx = lax.rem(block_of(kind, zh, core) - x + 4, 4)
    jy = lax.rem(yb - y + 4, 4)
    is0 = core == 0
    return (
        jnp.where(is0, jx, jy),
        jnp.where(is0, 4 * zl + yb, 4 * kind + zl),
    )


def rows_at(index, size, offset, count):
    return pl.ds(pl.multiple_of(index * size + offset, 8), count)


def emit(room, outs, sems):
    copies = [pltpu.make_async_copy(room.at[j], outs[j], sems.at[j]) for j in range(4)]
    for c in copies:
        c.start()
    for c in copies:
        c.wait()


def own_kernel(scalars, km, ko, vm, vo, *rest):
    outs, room, sems = rest[:4], rest[4], rest[5]
    for kind, (left, right) in enumerate([(km, km), (ko, km), (vm, vm), (vo, vm)]):
        for zl in range(4):
            block = product(left[:, 128 * zl : 128 * (zl + 1)], right[...])
            for yb in range(4):
                part, i = place(scalars, kind, zl, yb)
                for cg in range(4):
                    room[part, rows_at(i, 128, 32 * cg, 32), :] = block[
                        32 * yb : 32 * (yb + 1), 128 * cg : 128 * (cg + 1)
                    ]
    emit(room, outs, sems)


def cross_kernel(latent, scalars, nm, no, *rest):
    fars, outs, room, sems = rest[:-6], rest[-6:-2], rest[-2], rest[-1]
    size, e = room.shape[1] // 16, 0
    if latent:
        lefts, fars = fars[:4], fars[4:]
        for kind, left in enumerate(lefts):
            block = product(left[...], lefts[0][...])
            for zl in range(4):
                for yb in range(4):
                    part, i = place(scalars, kind, zl, yb)
                    row = 32 * zl + 8 * yb
                    room[part, rows_at(i, size, size - 8, 8), :] = block[row : row + 8, :]
    for far in fars:
        quarters = far.shape[1] // 128
        for kind, near in enumerate([nm, no]):
            for zl in range(4):
                block = product(near[:, 128 * zl : 128 * (zl + 1)], far[...])
                for yb in range(4):
                    part, i = place(scalars, kind, zl, yb)
                    for q in range(quarters):
                        room[part, rows_at(i, size, 32 * (e + q), 32), :] = block[
                            32 * yb : 32 * (yb + 1), 128 * q : 128 * (q + 1)
                        ]
            for q in range(quarters):
                block = product(far[:, 128 * q : 128 * (q + 1)], near[...])
                for zl in range(4):
                    for yb in range(4):
                        part, i = place(scalars, kind + 2, zl, yb)
                        row = 32 * zl + 8 * yb
                        for cg in range(4):
                            at = 32 * (e + q) + 8 * cg
                            room[part, rows_at(i, size, at, 8), :] = block[
                                row : row + 8, 128 * cg : 128 * (cg + 1)
                            ]
        e += quarters
    emit(room, outs, sems)


def middle_kernel(sizes, gathered, scalars, *refs):
    x, y, zh, core = scalars[0], scalars[1], scalars[3], scalars[4]
    ins, outs = refs[:-4], refs[-4:]
    if gathered:
        piece, ins = ins[-1], ins[:-1]
    each = len(ins) // len(sizes)
    is0 = core == 0
    whole = sum(sizes)
    for j, out in enumerate(outs):
        yb = lax.rem(y + j, 4)
        xb = lax.rem(x + j, 4)
        kind = 2 * jnp.where(xb // 2 == zh, 0, 1) + jnp.where(xb % 2 == core, 0, 1)
        for slab in range(4):
            index = jnp.where(is0, 4 * slab + yb, 4 * kind + slab)
            start = whole * slab
            for n, size in enumerate(sizes):
                at = rows_at(index, size, 0, size)
                total = ins[each * n][at]
                for r in ins[each * n + 1 : each * (n + 1)]:
                    total += r[at]
                out[start : start + size] = total
                start += size
        if gathered:
            out[4 * whole : 4 * whole + 8] = piece[...]


def last_kernel(size, gathered, scalars, a, b, c, d, *outs):
    zl = scalars[2]
    for j, out in enumerate(outs):
        at = rows_at(lax.rem(zl + j, 4), size, 0, size)
        out[:size] = (a[at] + b[at]) + (c[at] + d[at])
        if gathered:
            for n, r in enumerate((a, b, c, d)):
                out[size + 8 * n : size + 8 * (n + 1)] = r[4 * size : 4 * size + 8]


def latent_kernel(scale, scalars, a, b, c, d, out):
    x, y, zl, core = scalars[0], scalars[1], scalars[2], scalars[4]
    is0 = core == 0
    for j1, ref in enumerate((a, b, c, d)):
        for jz in range(4):
            for j2 in range(4):
                xb = lax.rem(x + 4 - jnp.where(is0, j1, j2), 4)
                yb = lax.rem(y + 4 - jnp.where(is0, j2, j1), 4)
                zb = lax.rem(zl + 4 - jz, 4)
                to = rows_at(16 * xb + 4 * zb + yb, 8, 0, 8)
                at = 32 * jz + 8 * j2
                out[to, :] = ref[at : at + 8, :] * scale


def finish_kernel(scale, scalars, own, cross, moved, turned, order, key_out, value_out):
    x, zh, core = scalars[0], scalars[3], scalars[4]
    inside = x // 2 == zh

    @pl.when(inside)
    def _():
        for cg in range(4):
            key_out[:, 128 * cg : 128 * (cg + 1)] = own[32 * cg : 32 * (cg + 1)] * scale
            value_out[:, 128 * cg : 128 * (cg + 1)] = moved[32 * cg : 32 * (cg + 1)] * scale

    @pl.when(jnp.logical_not(inside))
    def _():
        back = jnp.zeros(key_out.shape, F32)
        for e in range(4):
            rest = moved[32 * e : 32 * (e + 1)] * scale
            for _ in range(3):
                top = rest.astype(jnp.bfloat16)
                back += jnp.dot(top, order[128 * e : 128 * (e + 1)], preferred_element_type=F32)
                rest -= top.astype(F32)

        here = lax.rem(x, 2) == core

        def stay_to(out):
            for e in range(4):
                for cg in range(4):
                    at = 32 * e + 8 * cg
                    tile = jnp.where(here, cross[at : at + 8], turned[at : at + 8])
                    out[8 * e : 8 * (e + 1), 128 * cg : 128 * (cg + 1)] = tile * scale

        @pl.when(zh == 0)
        def _():
            stay_to(key_out)
            value_out[...] = back

        @pl.when(zh == 1)
        def _():
            key_out[...] = back
            stay_to(value_out)


SMEM = pl.BlockSpec(memory_space=pltpu.SMEM)
VMEM = pl.BlockSpec(memory_space=pltpu.VMEM)
ANY = pl.BlockSpec(memory_space=pl.ANY)
LIMIT = pltpu.CompilerParams(vmem_limit_bytes=40 * 2**20)


def blocks_call(kernel, rows, scalars, *operands):
    outs = [jax.ShapeDtypeStruct((rows, 128), F32)] * 4
    return pl.pallas_call(
        kernel,
        out_shape=outs,
        in_specs=[SMEM] + [VMEM] * len(operands),
        out_specs=[ANY] * len(outs),
        scratch_shapes=[pltpu.VMEM((4, rows, 128), F32), pltpu.SemaphoreType.DMA((len(outs),))],
        compiler_params=LIMIT,
        cost_estimate=pl.CostEstimate(flops=0, bytes_accessed=0, transcendentals=0),
    )(scalars, *operands)


def sums_call(kernel, shapes, scalars, *operands):
    outs = [jax.ShapeDtypeStruct(s, F32) for s in shapes]
    head = [] if scalars is None else [scalars]
    return pl.pallas_call(
        kernel,
        out_shape=outs,
        in_specs=[SMEM] * len(head) + [VMEM] * len(operands),
        out_specs=[VMEM] * len(outs),
        compiler_params=LIMIT,
        cost_estimate=pl.CostEstimate(flops=0, bytes_accessed=0, transcendentals=0),
    )(*head, *operands)


def exchange(parts, direction):
    return [parts[0]] + [move(parts[j], direction(j)) for j in (1, 2, 3)]


def after(value, *others):
    return lax.optimization_barrier((value,) + others)[0]


def shards(latent, grad_key, grad_value):
    x, zl, y, zh, core = (lax.axis_index(a) for a in AXES)
    scalars = jnp.stack([x, y, zl, zh, core]).astype(jnp.int32)
    scale = 1.0 / (latent.shape[0] * 64)
    width = grad_key.shape[1]
    low = zh == 0

    to = jnp.arange(width)
    source = 128 * ((to // 32) % 4) + 32 * ((to // 8) % 4) + 8 * (to // 128) + to % 8
    order = (source[:, None] == jnp.arange(width)[None, :]).astype(jnp.bfloat16)
    chosen = jnp.where(low, grad_value, grad_key)
    ordered, start = [], 0
    for quarters in CHUNKS:
        pick = (jnp.arange(width)[:, None] == source[None, start : start + 128 * quarters])
        part = jnp.dot(chosen, pick.astype(jnp.bfloat16), preferred_element_type=F32)
        ordered.append(part.astype(jnp.bfloat16))
        start += 128 * quarters
    latent_far = move(latent, to_half)
    far0 = move(ordered[0], to_half)
    far1 = move(ordered[1], to_half)

    key_other = move(grad_key, to_core)
    value_other = move(grad_value, to_core)
    latent_other = move(latent, to_core)
    near = jnp.where(low, grad_key, grad_value)
    near_other = jnp.where(low, key_other, value_other)

    def middle(sizes, *parts, gathered=False, gate):
        shape = (4 * sum(sizes) + (8 if gathered else 0), 128)
        kernel = functools.partial(middle_kernel, sizes, gathered)
        return sums_call(kernel, [shape] * 4, after(scalars, gate), *parts)

    def last(size, *parts, gathered=False, gate=()):
        shape = (size + (32 if gathered else 0), 128)
        kernel = functools.partial(last_kernel, size, gathered)
        return sums_call(kernel, [shape] * 4, after(scalars, gate), *parts)

    own = blocks_call(
        own_kernel, 16 * 128, scalars, grad_key, key_other, grad_value, value_other
    )
    gate = own[0]
    own = exchange(own, first)

    latent_far_other = move(latent_far, to_core)
    c0 = blocks_call(
        functools.partial(cross_kernel, True), 16 * 40, after(scalars, gate), near, near_other,
        latent, latent_other, latent_far, latent_far_other, far0,
    )
    c1 = blocks_call(
        functools.partial(cross_kernel, False), 16 * 96, after(scalars, c0[0]), near, near_other, far1
    )
    c0 = exchange(c0, first)
    c0 = middle((128, 40), *own, *c0, gate=c1[0])
    c1 = exchange(c1, first)
    c0 = exchange(c0, second)
    c0 = exchange(last(168, *c0), along_z)
    c0 = (c0[0] + c0[1]) + (c0[2] + c0[3])
    own = c0[:128]
    c = middle((96,), *c1, c0[160:], gathered=True, gate=c0)
    c = exchange(c, second)
    c = exchange(last(96, *c, gathered=True), along_z)
    pieces = jnp.concatenate([part[96:] for part in c], axis=0)
    ends = (c[0][:96] + c[1][:96]) + (c[2][:96] + c[3][:96])
    crossed = jnp.concatenate([c0[128:160], ends], axis=0)
    moved = move(jnp.where(x // 2 == zh, crossed, own), homeward)
    turned = move(crossed, sideways)
    (latent_sum,) = sums_call(
        functools.partial(latent_kernel, scale), [(512, 128)], scalars, *exchange([pieces] * 4, first)
    )
    key_sum, value_sum = sums_call(
        functools.partial(finish_kernel, scale), [(32, width)] * 2, scalars, own, crossed, moved, turned, order
    )
    return latent_sum, key_sum, value_sum


def solution(mesh):
    fine = Mesh(mesh.devices.reshape(SIZES), AXES)
    tok, proj = ("x", "zl", "y"), ("zh", "core")
    placed = (P(tok, proj), P(tok, proj), P(tok, proj))
    return jax.shard_map(
        shards,
        mesh=fine,
        in_specs=placed,
        out_specs=(P(None, proj), P(tok, proj), P(tok, proj)),
        check_vma=False,
    )
```

```python
import functools
import itertools

import jax
import jax.numpy as jnp
from jax import lax
from jax.experimental import pallas as pl
from jax.experimental.pallas import tpu as pltpu
from jax.sharding import Mesh, PartitionSpec as P

AXES = ("x", "zl", "y", "zh", "core")
SIZES = (4, 4, 4, 2, 2)
CHUNKS = (1, 3)
F32 = jnp.float32


def move(values, where):
    pairs = []
    for source, place in enumerate(itertools.product(*[range(n) for n in SIZES])):
        target = where(*place)
        if target is None:
            continue
        index = 0
        for n, t in zip(SIZES, target):
            index = index * n + t % n
        pairs.append((source, index))
    return lax.ppermute(values, AXES, pairs)


def to_core(x, zl, y, zh, core):
    return (x, zl, y, zh, 1 - core)


def to_half(x, zl, y, zh, core):
    return (x, zl, y, 1 - zh, core)


def first(step):
    return lambda x, zl, y, zh, core: (
        (x + step, zl, y, zh, core) if core == 0 else (x, zl, y + step, zh, core)
    )


def second(step):
    return lambda x, zl, y, zh, core: (
        (x, zl, y + step, zh, core) if core == 0 else (x + step, zl, y, zh, core)
    )


def along_z(step):
    return lambda x, zl, y, zh, core: (x, zl + step, y, zh, core)


def homeward(x, zl, y, zh, core):
    return (x, zl, y, 1 - zh, core) if x // 2 == zh else (x + 2, zl, y, zh, core)


def sideways(x, zl, y, zh, core):
    return (x ^ 1, zl, y, zh, 1 - core) if x // 2 != zh and x % 2 != core else None


def product(left, right):
    return lax.dot_general(left, right, (((0,), (0,)), ((), ())), preferred_element_type=F32)


def block_of(kind, zh, core):
    half = zh if kind < 2 else 1 - zh
    return 2 * half + (core if kind % 2 == 0 else 1 - core)


def place(scalars, kind, zl, yb):
    x, y, zh, core = scalars[0], scalars[1], scalars[3], scalars[4]
    jx = lax.rem(block_of(kind, zh, core) - x + 4, 4)
    jy = lax.rem(yb - y + 4, 4)
    is0 = core == 0
    return (
        jnp.where(is0, jx, jy),
        jnp.where(is0, 4 * zl + yb, 4 * kind + zl),
    )


def rows_at(index, size, offset, count):
    return pl.ds(pl.multiple_of(index * size + offset, 8), count)


def emit(room, outs, sems):
    copies = [pltpu.make_async_copy(room.at[j], outs[j], sems.at[j]) for j in range(4)]
    for c in copies:
        c.start()
    for c in copies:
        c.wait()


def own_kernel(scalars, km, ko, vm, vo, *rest):
    outs, room, sems = rest[:4], rest[4], rest[5]
    for kind, (left, right) in enumerate([(km, km), (ko, km), (vm, vm), (vo, vm)]):
        for zl in range(4):
            block = product(left[:, 128 * zl : 128 * (zl + 1)], right[...])
            for yb in range(4):
                part, i = place(scalars, kind, zl, yb)
                for cg in range(4):
                    room[part, rows_at(i, 128, 32 * cg, 32), :] = block[
                        32 * yb : 32 * (yb + 1), 128 * cg : 128 * (cg + 1)
                    ]
    emit(room, outs, sems)


def cross_kernel(latent, scalars, nm, no, *rest):
    fars, outs, room, sems = rest[:-6], rest[-6:-2], rest[-2], rest[-1]
    size, e = room.shape[1] // 16, 0
    if latent:
        lefts, fars = fars[:4], fars[4:]
        for kind, left in enumerate(lefts):
            block = product(left[...], lefts[0][...])
            for zl in range(4):
                for yb in range(4):
                    part, i = place(scalars, kind, zl, yb)
                    row = 32 * zl + 8 * yb
                    room[part, rows_at(i, size, size - 8, 8), :] = block[row : row + 8, :]
    for far in fars:
        quarters = far.shape[1] // 128
        for kind, near in enumerate([nm, no]):
            for zl in range(4):
                block = product(near[:, 128 * zl : 128 * (zl + 1)], far[...])
                for yb in range(4):
                    part, i = place(scalars, kind, zl, yb)
                    for q in range(quarters):
                        room[part, rows_at(i, size, 32 * (e + q), 32), :] = block[
                            32 * yb : 32 * (yb + 1), 128 * q : 128 * (q + 1)
                        ]
            for q in range(quarters):
                block = product(far[:, 128 * q : 128 * (q + 1)], near[...])
                for zl in range(4):
                    for yb in range(4):
                        part, i = place(scalars, kind + 2, zl, yb)
                        row = 32 * zl + 8 * yb
                        for cg in range(4):
                            at = 32 * (e + q) + 8 * cg
                            room[part, rows_at(i, size, at, 8), :] = block[
                                row : row + 8, 128 * cg : 128 * (cg + 1)
                            ]
        e += quarters
    emit(room, outs, sems)


def middle_kernel(sizes, scalars, *refs):
    x, y, zh, core = scalars[0], scalars[1], scalars[3], scalars[4]
    ins, outs = refs[:-4], refs[-4:]
    each = len(ins) // len(sizes)
    is0 = core == 0
    whole = sum(sizes)
    for j, out in enumerate(outs):
        yb = lax.rem(y + j, 4)
        xb = lax.rem(x + j, 4)
        kind = 2 * jnp.where(xb // 2 == zh, 0, 1) + jnp.where(xb % 2 == core, 0, 1)
        for slab in range(4):
            index = jnp.where(is0, 4 * slab + yb, 4 * kind + slab)
            start = whole * slab
            for n, size in enumerate(sizes):
                at = rows_at(index, size, 0, size)
                total = ins[each * n][at]
                for r in ins[each * n + 1 : each * (n + 1)]:
                    total += r[at]
                out[start : start + size] = total
                start += size


def last_kernel(size, scalars, a, b, c, d, *rest):
    zl = scalars[2]
    more, outs = rest[:-4], rest[-4:]
    for j, out in enumerate(outs):
        at = rows_at(lax.rem(zl + j, 4), size, 0, size)
        out[:size] = (a[at] + b[at]) + (c[at] + d[at])
        for piece in more:
            out[size:] = piece[...]


def latent_kernel(scale, scalars, a, b, c, d, out):
    x, y, zl, core = scalars[0], scalars[1], scalars[2], scalars[4]
    is0 = core == 0
    for j2, ref in enumerate((a, b, c, d)):
        for j1 in range(4):
            for jz in range(4):
                xb = lax.rem(x + 4 - jnp.where(is0, j1, j2), 4)
                yb = lax.rem(y + 4 - jnp.where(is0, j2, j1), 4)
                zb = lax.rem(zl + 4 - jz, 4)
                to = rows_at(16 * xb + 4 * zb + yb, 8, 0, 8)
                at = 32 * j1 + 8 * jz
                out[to, :] = ref[at : at + 8, :] * scale


def finish_kernel(scale, scalars, own, cross, moved, turned, order, key_out, value_out):
    x, zh, core = scalars[0], scalars[3], scalars[4]
    inside = x // 2 == zh

    @pl.when(inside)
    def _():
        for cg in range(4):
            key_out[:, 128 * cg : 128 * (cg + 1)] = own[32 * cg : 32 * (cg + 1)] * scale
            value_out[:, 128 * cg : 128 * (cg + 1)] = moved[32 * cg : 32 * (cg + 1)] * scale

    @pl.when(jnp.logical_not(inside))
    def _():
        back = jnp.zeros(key_out.shape, F32)
        for e in range(4):
            rest = moved[32 * e : 32 * (e + 1)] * scale
            for _ in range(3):
                top = rest.astype(jnp.bfloat16)
                back += jnp.dot(top, order[128 * e : 128 * (e + 1)], preferred_element_type=F32)
                rest -= top.astype(F32)

        here = lax.rem(x, 2) == core

        def stay_to(out):
            for e in range(4):
                for cg in range(4):
                    at = 32 * e + 8 * cg
                    tile = jnp.where(here, cross[at : at + 8], turned[at : at + 8])
                    out[8 * e : 8 * (e + 1), 128 * cg : 128 * (cg + 1)] = tile * scale

        @pl.when(zh == 0)
        def _():
            stay_to(key_out)
            value_out[...] = back

        @pl.when(zh == 1)
        def _():
            key_out[...] = back
            stay_to(value_out)


SMEM = pl.BlockSpec(memory_space=pltpu.SMEM)
VMEM = pl.BlockSpec(memory_space=pltpu.VMEM)
ANY = pl.BlockSpec(memory_space=pl.ANY)
LIMIT = pltpu.CompilerParams(vmem_limit_bytes=40 * 2**20)


def blocks_call(kernel, rows, scalars, *operands):
    outs = [jax.ShapeDtypeStruct((rows, 128), F32)] * 4
    return pl.pallas_call(
        kernel,
        out_shape=outs,
        in_specs=[SMEM] + [VMEM] * len(operands),
        out_specs=[ANY] * len(outs),
        scratch_shapes=[pltpu.VMEM((4, rows, 128), F32), pltpu.SemaphoreType.DMA((len(outs),))],
        compiler_params=LIMIT,
        cost_estimate=pl.CostEstimate(flops=0, bytes_accessed=0, transcendentals=0),
    )(scalars, *operands)


def sums_call(kernel, shapes, scalars, *operands):
    outs = [jax.ShapeDtypeStruct(s, F32) for s in shapes]
    head = [] if scalars is None else [scalars]
    return pl.pallas_call(
        kernel,
        out_shape=outs,
        in_specs=[SMEM] * len(head) + [VMEM] * len(operands),
        out_specs=[VMEM] * len(outs),
        compiler_params=LIMIT,
        cost_estimate=pl.CostEstimate(flops=0, bytes_accessed=0, transcendentals=0),
    )(*head, *operands)


def exchange(parts, direction):
    return [parts[0]] + [move(parts[j], direction(j)) for j in (1, 2, 3)]


def after(value, *others):
    return lax.optimization_barrier((value,) + others)[0]


def shards(latent, grad_key, grad_value):
    x, zl, y, zh, core = (lax.axis_index(a) for a in AXES)
    scalars = jnp.stack([x, y, zl, zh, core]).astype(jnp.int32)
    scale = 1.0 / (latent.shape[0] * 64)
    width = grad_key.shape[1]
    low = zh == 0

    to = jnp.arange(width)
    source = 128 * ((to // 32) % 4) + 32 * ((to // 8) % 4) + 8 * (to // 128) + to % 8
    order = (source[:, None] == jnp.arange(width)[None, :]).astype(jnp.bfloat16)
    chosen = jnp.where(low, grad_value, grad_key)
    ordered, start = [], 0
    for quarters in CHUNKS:
        pick = (jnp.arange(width)[:, None] == source[None, start : start + 128 * quarters])
        part = jnp.dot(chosen, pick.astype(jnp.bfloat16), preferred_element_type=F32)
        ordered.append(part.astype(jnp.bfloat16))
        start += 128 * quarters
    latent_far = move(latent, to_half)
    far0 = move(ordered[0], to_half)
    far1 = move(ordered[1], to_half)

    key_other = move(grad_key, to_core)
    value_other = move(grad_value, to_core)
    latent_other = move(latent, to_core)
    near = jnp.where(low, grad_key, grad_value)
    near_other = jnp.where(low, key_other, value_other)

    def middle(sizes, *parts, gate):
        kernel = functools.partial(middle_kernel, sizes)
        return sums_call(kernel, [(4 * sum(sizes), 128)] * 4, after(scalars, gate), *parts)

    def last(size, *parts):
        rows = size + sum(p.shape[0] for p in parts[4:])
        return sums_call(functools.partial(last_kernel, size), [(rows, 128)] * 4, scalars, *parts)

    own = blocks_call(
        own_kernel, 16 * 128, scalars, grad_key, key_other, grad_value, value_other
    )
    gate = own[0]
    own = exchange(own, first)

    latent_far_other = move(latent_far, to_core)
    c0 = blocks_call(
        functools.partial(cross_kernel, True), 16 * 40, after(scalars, gate), near, near_other,
        latent, latent_other, latent_far, latent_far_other, far0,
    )
    c1 = blocks_call(
        functools.partial(cross_kernel, False), 16 * 96, after(scalars, c0[0]), near, near_other, far1
    )
    c0 = exchange(c0, first)
    c0 = middle((128, 40), *own, *c0, gate=c1[0])
    c1 = exchange(c1, first)
    c0 = exchange(c0, second)
    c0 = exchange(last(168, *c0), along_z)
    c0 = (c0[0] + c0[1]) + (c0[2] + c0[3])
    own = c0[:128]
    c = middle((96,), *c1, gate=gate)
    c = exchange(c, second)
    c = exchange(last(96, *c, c0[160:]), along_z)
    pieces = jnp.concatenate([part[96:] for part in c], axis=0)
    ends = (c[0][:96] + c[1][:96]) + (c[2][:96] + c[3][:96])
    crossed = jnp.concatenate([c0[128:160], ends], axis=0)
    pieces = jnp.concatenate(exchange([pieces] * 4, first), axis=0)
    moved = move(jnp.where(x // 2 == zh, crossed, own), homeward)
    turned = move(crossed, sideways)
    (latent_sum,) = sums_call(
        functools.partial(latent_kernel, scale), [(512, 128)], scalars, *exchange([pieces] * 4, second)
    )
    key_sum, value_sum = sums_call(
        functools.partial(finish_kernel, scale), [(32, width)] * 2, scalars, own, crossed, moved, turned, order
    )
    return latent_sum, key_sum, value_sum


def solution(mesh):
    fine = Mesh(mesh.devices.reshape(SIZES), AXES)
    tok, proj = ("x", "zl", "y"), ("zh", "core")
    placed = (P(tok, proj), P(tok, proj), P(tok, proj))
    return jax.shard_map(
        shards,
        mesh=fine,
        in_specs=placed,
        out_specs=(P(None, proj), P(tok, proj), P(tok, proj)),
        check_vma=False,
    )
```

```python
import functools
import itertools

import jax
import jax.numpy as jnp
from jax import lax
from jax.experimental import pallas as pl
from jax.experimental.pallas import tpu as pltpu
from jax.sharding import Mesh, PartitionSpec as P

AXES = ("x", "zl", "y", "zh", "core")
SIZES = (4, 4, 4, 2, 2)
CHUNKS = (1, 3)
F32 = jnp.float32


def move(values, where):
    pairs = []
    for source, place in enumerate(itertools.product(*[range(n) for n in SIZES])):
        target = where(*place)
        if target is None:
            continue
        index = 0
        for n, t in zip(SIZES, target):
            index = index * n + t % n
        pairs.append((source, index))
    return lax.ppermute(values, AXES, pairs)


def to_core(x, zl, y, zh, core):
    return (x, zl, y, zh, 1 - core)


def to_half(x, zl, y, zh, core):
    return (x, zl, y, 1 - zh, core)


def first(step):
    return lambda x, zl, y, zh, core: (
        (x + step, zl, y, zh, core) if core == 0 else (x, zl, y + step, zh, core)
    )


def second(step):
    return lambda x, zl, y, zh, core: (
        (x, zl, y + step, zh, core) if core == 0 else (x + step, zl, y, zh, core)
    )


def along_z(step):
    return lambda x, zl, y, zh, core: (x, zl + step, y, zh, core)


def homeward(x, zl, y, zh, core):
    return (x, zl, y, 1 - zh, core) if x // 2 == zh else (x + 2, zl, y, zh, core)


def sideways(x, zl, y, zh, core):
    return (x ^ 1, zl, y, zh, 1 - core) if x // 2 != zh and x % 2 != core else None


def product(left, right):
    return lax.dot_general(left, right, (((0,), (0,)), ((), ())), preferred_element_type=F32)


def block_of(kind, zh, core):
    half = zh if kind < 2 else 1 - zh
    return 2 * half + (core if kind % 2 == 0 else 1 - core)


def place(scalars, kind, zl, yb):
    x, y, zh, core = scalars[0], scalars[1], scalars[3], scalars[4]
    jx = lax.rem(block_of(kind, zh, core) - x + 4, 4)
    jy = lax.rem(yb - y + 4, 4)
    is0 = core == 0
    return (
        jnp.where(is0, jx, jy),
        jnp.where(is0, 4 * zl + yb, 4 * kind + zl),
    )


def rows_at(index, size, offset, count):
    return pl.ds(pl.multiple_of(index * size + offset, 8), count)


def emit(room, outs, sems):
    copies = [pltpu.make_async_copy(room.at[j], outs[j], sems.at[j]) for j in range(4)]
    for c in copies:
        c.start()
    for c in copies:
        c.wait()


def own_kernel(scalars, km, ko, vm, vo, *rest):
    outs, room, sems = rest[:4], rest[4], rest[5]
    for kind, (left, right) in enumerate([(km, km), (ko, km), (vm, vm), (vo, vm)]):
        for zl in range(4):
            block = product(left[:, 128 * zl : 128 * (zl + 1)], right[...])
            for yb in range(4):
                part, i = place(scalars, kind, zl, yb)
                for cg in range(4):
                    room[part, rows_at(i, 128, 32 * cg, 32), :] = block[
                        32 * yb : 32 * (yb + 1), 128 * cg : 128 * (cg + 1)
                    ]
    emit(room, outs, sems)


def cross_kernel(latent, scalars, nm, no, *rest):
    fars, outs, room, sems = rest[:-6], rest[-6:-2], rest[-2], rest[-1]
    size, e = room.shape[1] // 16, 0
    if latent:
        lefts, fars = fars[:4], fars[4:]
        for kind, left in enumerate(lefts):
            block = product(left[...], lefts[0][...])
            for zl in range(4):
                for yb in range(4):
                    part, i = place(scalars, kind, zl, yb)
                    row = 32 * zl + 8 * yb
                    room[part, rows_at(i, size, size - 8, 8), :] = block[row : row + 8, :]
    for far in fars:
        quarters = far.shape[1] // 128
        for kind, near in enumerate([nm, no]):
            for zl in range(4):
                block = product(near[:, 128 * zl : 128 * (zl + 1)], far[...])
                for yb in range(4):
                    part, i = place(scalars, kind, zl, yb)
                    for q in range(quarters):
                        room[part, rows_at(i, size, 32 * (e + q), 32), :] = block[
                            32 * yb : 32 * (yb + 1), 128 * q : 128 * (q + 1)
                        ]
            for q in range(quarters):
                block = product(far[:, 128 * q : 128 * (q + 1)], near[...])
                for zl in range(4):
                    for yb in range(4):
                        part, i = place(scalars, kind + 2, zl, yb)
                        row = 32 * zl + 8 * yb
                        for cg in range(4):
                            at = 32 * (e + q) + 8 * cg
                            room[part, rows_at(i, size, at, 8), :] = block[
                                row : row + 8, 128 * cg : 128 * (cg + 1)
                            ]
        e += quarters
    emit(room, outs, sems)


def middle_kernel(sizes, scalars, *refs):
    x, y, zh, core = scalars[0], scalars[1], scalars[3], scalars[4]
    ins, outs = refs[:-4], refs[-4:]
    each = len(ins) // len(sizes)
    is0 = core == 0
    whole = sum(sizes)
    for j, out in enumerate(outs):
        yb = lax.rem(y + j, 4)
        xb = lax.rem(x + j, 4)
        kind = 2 * jnp.where(xb // 2 == zh, 0, 1) + jnp.where(xb % 2 == core, 0, 1)
        for slab in range(4):
            index = jnp.where(is0, 4 * slab + yb, 4 * kind + slab)
            start = whole * slab
            for n, size in enumerate(sizes):
                at = rows_at(index, size, 0, size)
                total = ins[each * n][at]
                for r in ins[each * n + 1 : each * (n + 1)]:
                    total += r[at]
                out[start : start + size] = total
                start += size


def last_kernel(scalars, a, b, c, d, e, f, g, h, *outs):
    zl = scalars[2]
    for j, out in enumerate(outs):
        i = lax.rem(zl + j, 4)
        at = rows_at(i, 168, 0, 160)
        out[:160] = (a[at] + b[at]) + (c[at] + d[at])
        for slab in range(4):
            at = pl.ds(168 * slab + 160, 8)
            out[160 + 8 * slab : 168 + 8 * slab] = (a[at] + b[at]) + (c[at] + d[at])
        at = rows_at(i, 96, 0, 96)
        out[192:] = (e[at] + f[at]) + (g[at] + h[at])


def latent_kernel(scale, scalars, a, b, c, d, out):
    x, y, core = scalars[0], scalars[1], scalars[4]
    is0 = core == 0
    for j2, ref in enumerate((a, b, c, d)):
        for j1 in range(4):
            for zb in range(4):
                xb = lax.rem(x + 4 - jnp.where(is0, j1, j2), 4)
                yb = lax.rem(y + 4 - jnp.where(is0, j2, j1), 4)
                to = rows_at(16 * xb + 4 * zb + yb, 8, 0, 8)
                at = 32 * j1 + 8 * zb
                out[to, :] = ref[at : at + 8, :] * scale


def finish_kernel(scale, scalars, own, cross, moved, turned, order, key_out, value_out):
    x, zh, core = scalars[0], scalars[3], scalars[4]
    inside = x // 2 == zh

    @pl.when(inside)
    def _():
        for cg in range(4):
            key_out[:, 128 * cg : 128 * (cg + 1)] = own[32 * cg : 32 * (cg + 1)] * scale
            value_out[:, 128 * cg : 128 * (cg + 1)] = moved[32 * cg : 32 * (cg + 1)] * scale

    @pl.when(jnp.logical_not(inside))
    def _():
        back = jnp.zeros(key_out.shape, F32)
        for e in range(4):
            rest = moved[32 * e : 32 * (e + 1)] * scale
            for _ in range(3):
                top = rest.astype(jnp.bfloat16)
                back += jnp.dot(top, order[128 * e : 128 * (e + 1)], preferred_element_type=F32)
                rest -= top.astype(F32)

        here = lax.rem(x, 2) == core

        def stay_to(out):
            for e in range(4):
                for cg in range(4):
                    at = 32 * e + 8 * cg
                    tile = jnp.where(here, cross[at : at + 8], turned[at : at + 8])
                    out[8 * e : 8 * (e + 1), 128 * cg : 128 * (cg + 1)] = tile * scale

        @pl.when(zh == 0)
        def _():
            stay_to(key_out)
            value_out[...] = back

        @pl.when(zh == 1)
        def _():
            key_out[...] = back
            stay_to(value_out)


SMEM = pl.BlockSpec(memory_space=pltpu.SMEM)
VMEM = pl.BlockSpec(memory_space=pltpu.VMEM)
ANY = pl.BlockSpec(memory_space=pl.ANY)
LIMIT = pltpu.CompilerParams(vmem_limit_bytes=40 * 2**20)


def blocks_call(kernel, rows, scalars, *operands):
    outs = [jax.ShapeDtypeStruct((rows, 128), F32)] * 4
    return pl.pallas_call(
        kernel,
        out_shape=outs,
        in_specs=[SMEM] + [VMEM] * len(operands),
        out_specs=[ANY] * len(outs),
        scratch_shapes=[pltpu.VMEM((4, rows, 128), F32), pltpu.SemaphoreType.DMA((len(outs),))],
        compiler_params=LIMIT,
        cost_estimate=pl.CostEstimate(flops=0, bytes_accessed=0, transcendentals=0),
    )(scalars, *operands)


def sums_call(kernel, shapes, scalars, *operands):
    outs = [jax.ShapeDtypeStruct(s, F32) for s in shapes]
    head = [] if scalars is None else [scalars]
    return pl.pallas_call(
        kernel,
        out_shape=outs,
        in_specs=[SMEM] * len(head) + [VMEM] * len(operands),
        out_specs=[VMEM] * len(outs),
        compiler_params=LIMIT,
        cost_estimate=pl.CostEstimate(flops=0, bytes_accessed=0, transcendentals=0),
    )(*head, *operands)


def exchange(parts, direction):
    return [parts[0]] + [move(parts[j], direction(j)) for j in (1, 2, 3)]


def after(value, *others):
    return lax.optimization_barrier((value,) + others)[0]


def shards(latent, grad_key, grad_value):
    x, zl, y, zh, core = (lax.axis_index(a) for a in AXES)
    scalars = jnp.stack([x, y, zl, zh, core]).astype(jnp.int32)
    scale = 1.0 / (latent.shape[0] * 64)
    width = grad_key.shape[1]
    low = zh == 0

    to = jnp.arange(width)
    source = 128 * ((to // 32) % 4) + 32 * ((to // 8) % 4) + 8 * (to // 128) + to % 8
    order = (source[:, None] == jnp.arange(width)[None, :]).astype(jnp.bfloat16)
    chosen = jnp.where(low, grad_value, grad_key)
    ordered, start = [], 0
    for quarters in CHUNKS:
        pick = (jnp.arange(width)[:, None] == source[None, start : start + 128 * quarters])
        part = jnp.dot(chosen, pick.astype(jnp.bfloat16), preferred_element_type=F32)
        ordered.append(part.astype(jnp.bfloat16))
        start += 128 * quarters
    latent_far = move(latent, to_half)
    far0 = move(ordered[0], to_half)
    far1 = move(ordered[1], to_half)

    key_other = move(grad_key, to_core)
    value_other = move(grad_value, to_core)
    latent_other = move(latent, to_core)
    near = jnp.where(low, grad_key, grad_value)
    near_other = jnp.where(low, key_other, value_other)

    def middle(sizes, *parts, gate):
        kernel = functools.partial(middle_kernel, sizes)
        return sums_call(kernel, [(4 * sum(sizes), 128)] * 4, after(scalars, gate), *parts)

    own = blocks_call(
        own_kernel, 16 * 128, scalars, grad_key, key_other, grad_value, value_other
    )
    gate = own[0]
    own = exchange(own, first)

    latent_far_other = move(latent_far, to_core)
    c0 = blocks_call(
        functools.partial(cross_kernel, True), 16 * 40, after(scalars, gate), near, near_other,
        latent, latent_other, latent_far, latent_far_other, far0,
    )
    c1 = blocks_call(
        functools.partial(cross_kernel, False), 16 * 96, after(scalars, c0[0]), near, near_other, far1
    )
    c0 = exchange(c0, first)
    c0 = middle((128, 40), *own, *c0, gate=c1[0])
    c1 = exchange(c1, first)
    c0 = exchange(c0, second)
    c = exchange(middle((96,), *c1, gate=gate), second)
    c = exchange(sums_call(last_kernel, [(288, 128)] * 4, scalars, *c0, *c), along_z)
    c = (c[0] + c[1]) + (c[2] + c[3])
    own, pieces = c[:128], c[160:192]
    crossed = jnp.concatenate([c[128:160], c[192:]], axis=0)
    pieces = jnp.concatenate(exchange([pieces] * 4, first), axis=0)
    moved = move(jnp.where(x // 2 == zh, crossed, own), homeward)
    turned = move(crossed, sideways)
    (latent_sum,) = sums_call(
        functools.partial(latent_kernel, scale), [(512, 128)], scalars, *exchange([pieces] * 4, second)
    )
    key_sum, value_sum = sums_call(
        functools.partial(finish_kernel, scale), [(32, width)] * 2, scalars, own, crossed, moved, turned, order
    )
    return latent_sum, key_sum, value_sum


def solution(mesh):
    fine = Mesh(mesh.devices.reshape(SIZES), AXES)
    tok, proj = ("x", "zl", "y"), ("zh", "core")
    placed = (P(tok, proj), P(tok, proj), P(tok, proj))
    return jax.shard_map(
        shards,
        mesh=fine,
        in_specs=placed,
        out_specs=(P(None, proj), P(tok, proj), P(tok, proj)),
        check_vma=False,
    )
```

```python
import functools
import itertools

import jax
import jax.numpy as jnp
from jax import lax
from jax.experimental import pallas as pl
from jax.experimental.pallas import tpu as pltpu
from jax.sharding import Mesh, PartitionSpec as P

AXES = ("x", "zl", "y", "zh", "core")
SIZES = (4, 4, 4, 2, 2)
CHUNKS = (1, 3)
F32 = jnp.float32


def move(values, where):
    pairs = []
    for source, place in enumerate(itertools.product(*[range(n) for n in SIZES])):
        target = where(*place)
        if target is None:
            continue
        index = 0
        for n, t in zip(SIZES, target):
            index = index * n + t % n
        pairs.append((source, index))
    return lax.ppermute(values, AXES, pairs)


def to_core(x, zl, y, zh, core):
    return (x, zl, y, zh, 1 - core)


def to_half(x, zl, y, zh, core):
    return (x, zl, y, 1 - zh, core)


def first(step):
    return lambda x, zl, y, zh, core: (
        (x + step, zl, y, zh, core) if core == 0 else (x, zl, y + step, zh, core)
    )


def second(step):
    return lambda x, zl, y, zh, core: (
        (x, zl, y + step, zh, core) if core == 0 else (x + step, zl, y, zh, core)
    )


def along_z(step):
    return lambda x, zl, y, zh, core: (x, zl + step, y, zh, core)


def homeward(x, zl, y, zh, core):
    return (x, zl, y, 1 - zh, core) if x // 2 == zh else (x + 2, zl, y, zh, core)


def sideways(x, zl, y, zh, core):
    return (x ^ 1, zl, y, zh, 1 - core) if x // 2 != zh and x % 2 != core else None


def product(left, right):
    return lax.dot_general(left, right, (((0,), (0,)), ((), ())), preferred_element_type=F32)


def block_of(kind, zh, core):
    half = zh if kind < 2 else 1 - zh
    return 2 * half + (core if kind % 2 == 0 else 1 - core)


def place(scalars, kind, zl, yb):
    x, y, zh, core = scalars[0], scalars[1], scalars[3], scalars[4]
    jx = lax.rem(block_of(kind, zh, core) - x + 4, 4)
    jy = lax.rem(yb - y + 4, 4)
    is0 = core == 0
    return (
        jnp.where(is0, jx, jy),
        jnp.where(is0, 4 * zl + yb, 4 * kind + zl),
    )


def rows_at(index, size, offset, count):
    return pl.ds(pl.multiple_of(index * size + offset, 8), count)


def emit(room, outs, sems):
    copies = [pltpu.make_async_copy(room.at[j], outs[j], sems.at[j]) for j in range(4)]
    for c in copies:
        c.start()
    for c in copies:
        c.wait()


def own_kernel(scalars, km, ko, vm, vo, *rest):
    outs, room, sems = rest[:4], rest[4], rest[5]
    for kind, (left, right) in enumerate([(km, km), (ko, km), (vm, vm), (vo, vm)]):
        for zl in range(4):
            block = product(left[:, 128 * zl : 128 * (zl + 1)], right[...])
            for yb in range(4):
                part, i = place(scalars, kind, zl, yb)
                for cg in range(4):
                    room[part, rows_at(i, 128, 32 * cg, 32), :] = block[
                        32 * yb : 32 * (yb + 1), 128 * cg : 128 * (cg + 1)
                    ]
    emit(room, outs, sems)


def cross_kernel(latent, scalars, nm, no, *rest):
    fars, outs, room, sems = rest[:-6], rest[-6:-2], rest[-2], rest[-1]
    size, e = room.shape[1] // 16, 0
    if latent:
        lefts, fars = fars[:4], fars[4:]
        for kind, left in enumerate(lefts):
            block = product(left[...], lefts[0][...])
            for zl in range(4):
                for yb in range(4):
                    part, i = place(scalars, kind, zl, yb)
                    row = 32 * zl + 8 * yb
                    room[part, rows_at(i, size, size - 8, 8), :] = block[row : row + 8, :]
    for far in fars:
        quarters = far.shape[1] // 128
        for kind, near in enumerate([nm, no]):
            for zl in range(4):
                block = product(near[:, 128 * zl : 128 * (zl + 1)], far[...])
                for yb in range(4):
                    part, i = place(scalars, kind, zl, yb)
                    for q in range(quarters):
                        room[part, rows_at(i, size, 32 * (e + q), 32), :] = block[
                            32 * yb : 32 * (yb + 1), 128 * q : 128 * (q + 1)
                        ]
            for q in range(quarters):
                block = product(far[:, 128 * q : 128 * (q + 1)], near[...])
                for zl in range(4):
                    for yb in range(4):
                        part, i = place(scalars, kind + 2, zl, yb)
                        row = 32 * zl + 8 * yb
                        for cg in range(4):
                            at = 32 * (e + q) + 8 * cg
                            room[part, rows_at(i, size, at, 8), :] = block[
                                row : row + 8, 128 * cg : 128 * (cg + 1)
                            ]
        e += quarters
    emit(room, outs, sems)


def middle_kernel(sizes, scalars, *refs):
    x, y, zh, core = scalars[0], scalars[1], scalars[3], scalars[4]
    ins, outs = refs[:-4], refs[-4:]
    each = len(ins) // len(sizes)
    is0 = core == 0
    whole = sum(sizes)
    for j, out in enumerate(outs):
        yb = lax.rem(y + j, 4)
        xb = lax.rem(x + j, 4)
        kind = 2 * jnp.where(xb // 2 == zh, 0, 1) + jnp.where(xb % 2 == core, 0, 1)
        for slab in range(4):
            index = jnp.where(is0, 4 * slab + yb, 4 * kind + slab)
            start = whole * slab
            for n, size in enumerate(sizes):
                at = rows_at(index, size, 0, size)
                total = ins[each * n][at]
                for r in ins[each * n + 1 : each * (n + 1)]:
                    total += r[at]
                out[start : start + size] = total
                start += size


def last_kernel(scalars, a, b, c, d, e, f, g, h, *outs):
    zl = scalars[2]
    for j, out in enumerate(outs):
        i = lax.rem(zl + j, 4)
        at = rows_at(i, 168, 0, 160)
        out[:160] = (a[at] + b[at]) + (c[at] + d[at])
        for slab in range(4):
            at = pl.ds(168 * slab + 160, 8)
            out[160 + 8 * slab : 168 + 8 * slab] = (a[at] + b[at]) + (c[at] + d[at])
        at = rows_at(i, 96, 0, 96)
        out[192:] = (e[at] + f[at]) + (g[at] + h[at])


def latent_kernel(scale, scalars, a, b, c, d, out):
    x, y, core = scalars[0], scalars[1], scalars[4]
    is0 = core == 0
    for j2, ref in enumerate((a, b, c, d)):
        for j1 in range(4):
            for zb in range(4):
                xb = lax.rem(x + 4 - jnp.where(is0, j1, j2), 4)
                yb = lax.rem(y + 4 - jnp.where(is0, j2, j1), 4)
                to = rows_at(16 * xb + 4 * zb + yb, 8, 0, 8)
                at = 32 * j1 + 8 * zb
                out[to, :] = ref[at : at + 8, :] * scale


def finish_kernel(scale, scalars, own, cross, moved, turned, order, key_out, value_out):
    x, zh, core = scalars[0], scalars[3], scalars[4]
    inside = x // 2 == zh

    @pl.when(inside)
    def _():
        for cg in range(4):
            key_out[:, 128 * cg : 128 * (cg + 1)] = own[32 * cg : 32 * (cg + 1)] * scale
            value_out[:, 128 * cg : 128 * (cg + 1)] = moved[32 * cg : 32 * (cg + 1)] * scale

    @pl.when(jnp.logical_not(inside))
    def _():
        back = jnp.zeros(key_out.shape, F32)
        for e in range(4):
            rest = moved[32 * e : 32 * (e + 1)] * scale
            for _ in range(3):
                top = rest.astype(jnp.bfloat16)
                back += jnp.dot(top, order[128 * e : 128 * (e + 1)], preferred_element_type=F32)
                rest -= top.astype(F32)

        here = lax.rem(x, 2) == core

        def stay_to(out):
            for e in range(4):
                for cg in range(4):
                    at = 32 * e + 8 * cg
                    tile = jnp.where(here, cross[at : at + 8], turned[at : at + 8])
                    out[8 * e : 8 * (e + 1), 128 * cg : 128 * (cg + 1)] = tile * scale

        @pl.when(zh == 0)
        def _():
            stay_to(key_out)
            value_out[...] = back

        @pl.when(zh == 1)
        def _():
            key_out[...] = back
            stay_to(value_out)


SMEM = pl.BlockSpec(memory_space=pltpu.SMEM)
VMEM = pl.BlockSpec(memory_space=pltpu.VMEM)
ANY = pl.BlockSpec(memory_space=pl.ANY)
LIMIT = pltpu.CompilerParams(vmem_limit_bytes=40 * 2**20)


def blocks_call(kernel, rows, scalars, *operands):
    outs = [jax.ShapeDtypeStruct((rows, 128), F32)] * 4
    return pl.pallas_call(
        kernel,
        out_shape=outs,
        in_specs=[SMEM] + [VMEM] * len(operands),
        out_specs=[ANY] * len(outs),
        scratch_shapes=[pltpu.VMEM((4, rows, 128), F32), pltpu.SemaphoreType.DMA((len(outs),))],
        compiler_params=LIMIT,
        cost_estimate=pl.CostEstimate(flops=0, bytes_accessed=0, transcendentals=0),
    )(scalars, *operands)


def sums_call(kernel, shapes, scalars, *operands):
    outs = [jax.ShapeDtypeStruct(s, F32) for s in shapes]
    head = [] if scalars is None else [scalars]
    return pl.pallas_call(
        kernel,
        out_shape=outs,
        in_specs=[SMEM] * len(head) + [VMEM] * len(operands),
        out_specs=[VMEM] * len(outs),
        compiler_params=LIMIT,
        cost_estimate=pl.CostEstimate(flops=0, bytes_accessed=0, transcendentals=0),
    )(*head, *operands)


def exchange(parts, direction):
    return [parts[0]] + [move(parts[j], direction(j)) for j in (1, 2, 3)]


def after(value, *others):
    return lax.optimization_barrier((value,) + others)[0]


def shards(latent, grad_key, grad_value):
    x, zl, y, zh, core = (lax.axis_index(a) for a in AXES)
    scalars = jnp.stack([x, y, zl, zh, core]).astype(jnp.int32)
    scale = 1.0 / (latent.shape[0] * 64)
    width = grad_key.shape[1]
    low = zh == 0

    to = jnp.arange(width)
    source = 128 * ((to // 32) % 4) + 32 * ((to // 8) % 4) + 8 * (to // 128) + to % 8
    order = (source[:, None] == jnp.arange(width)[None, :]).astype(jnp.bfloat16)
    chosen = jnp.where(low, grad_value, grad_key)
    ordered, start = [], 0
    for quarters in CHUNKS:
        pick = (jnp.arange(width)[:, None] == source[None, start : start + 128 * quarters])
        part = jnp.dot(chosen, pick.astype(jnp.bfloat16), preferred_element_type=F32)
        ordered.append(part.astype(jnp.bfloat16))
        start += 128 * quarters
    latent_far = move(latent, to_half)
    far0 = move(ordered[0], to_half)
    far1 = move(ordered[1], to_half)

    key_other = move(grad_key, to_core)
    value_other = move(grad_value, to_core)
    latent_other = move(latent, to_core)
    near = jnp.where(low, grad_key, grad_value)
    near_other = jnp.where(low, key_other, value_other)

    def middle(sizes, *parts, gate):
        kernel = functools.partial(middle_kernel, sizes)
        return sums_call(kernel, [(4 * sum(sizes), 128)] * 4, after(scalars, gate), *parts)

    own = blocks_call(
        own_kernel, 16 * 128, scalars, grad_key, key_other, grad_value, value_other
    )
    gate = own[0]
    own = exchange(own, first)

    latent_far_other = move(latent_far, to_core)
    c0 = blocks_call(
        functools.partial(cross_kernel, True), 16 * 40, after(scalars, gate), near, near_other,
        latent, latent_other, latent_far, latent_far_other, far0,
    )
    c1 = blocks_call(
        functools.partial(cross_kernel, False), 16 * 96, after(scalars, c0[0]), near, near_other, far1
    )
    c0 = exchange(c0, first)
    c0 = middle((128, 40), *own, *c0, gate=c1[0])
    ready = c0[0]
    c1 = exchange(c1, first)
    c0 = exchange(c0, second)
    c = exchange(middle((96,), *c1, gate=ready), second)
    c = exchange(sums_call(last_kernel, [(288, 128)] * 4, scalars, *c0, *c), along_z)
    c = (c[0] + c[1]) + (c[2] + c[3])
    own, pieces = c[:128], c[160:192]
    crossed = jnp.concatenate([c[128:160], c[192:]], axis=0)
    pieces = jnp.concatenate(exchange([pieces] * 4, first), axis=0)
    moved = move(jnp.where(x // 2 == zh, crossed, own), homeward)
    turned = move(crossed, sideways)
    (latent_sum,) = sums_call(
        functools.partial(latent_kernel, scale), [(512, 128)], scalars, *exchange([pieces] * 4, second)
    )
    key_sum, value_sum = sums_call(
        functools.partial(finish_kernel, scale), [(32, width)] * 2, scalars, own, crossed, moved, turned, order
    )
    return latent_sum, key_sum, value_sum


def solution(mesh):
    fine = Mesh(mesh.devices.reshape(SIZES), AXES)
    tok, proj = ("x", "zl", "y"), ("zh", "core")
    placed = (P(tok, proj), P(tok, proj), P(tok, proj))
    return jax.shard_map(
        shards,
        mesh=fine,
        in_specs=placed,
        out_specs=(P(None, proj), P(tok, proj), P(tok, proj)),
        check_vma=False,
    )
```
